256 devices in a mesh: ka: 64 (over z, x, core), tau: 4 (over y).
Axes of the slice: x: 4, y: 4, z: 8, core: 2. Of those that a mesh axis runs over, the one named last changes fastest.
Arguments:
- green_forward: bfloat16 [64, 4, 512, 512], P('ka', 'tau'), may hold values from -12 to 12
- green_backward: bfloat16 [64, 4, 512, 512], P('ka', 'tau'), may hold values from -12 to 12
- orbitals: bfloat16 [64, 512, 2048], P('ka'), may hold values from -0.25 to 0.25
- difference_index_table: int32 [4, 64], replicated, may hold values from 0 to 63, as said below
- ir_matrix: float32 [4, 4], replicated, may hold values from -6 to 6
Outputs:
- polarization: bfloat16 [4, 4, 2048, 2048], P(None, None, 'ka', 'tau')
The draws below stay inside these ranges and needn't reach their ends.
Inputs may be any that keep to these rules, and one draw needn't show every extreme that they name: `difference_index_table`: row q is the map k -> k - s_q on a periodic cubic mesh of 64 momenta (k numbered with the last mesh dimension fastest), for a shift s_q of each row; every row is a permutation.
All inputs are finite; a program needn't handle non-finite values.
Results may differ from the reference program's by a relative error of at most 0.007.
Values may be sent and summed in bfloat16 or wider, within the bound.
A program may use at most 128 MiB of HBM per device.

```python
import jax
import jax.numpy as jnp
from jax import lax

NAO = 512
NAUX = 2048
NQ = 4
NW = 4
NK = 64
NTAU = 4


def draw_difference_index_table(key, part):
    key = jax.random.fold_in(key, 7)
    side = int(NK ** (1.0 / 3.0) + 0.5)
    shifts = jax.random.randint(key, (NQ, 3), 0, side)
    momenta = jnp.arange(NK, dtype=jnp.int32)
    first = momenta // (side * side)
    second = momenta // side % side
    third = momenta % side
    first_new = (first[None, :] - shifts[:, 0:1]) % side
    second_new = (second[None, :] - shifts[:, 1:2]) % side
    third_new = (third[None, :] - shifts[:, 2:3]) % side
    return ((first_new * side + second_new) * side + third_new).astype(jnp.int32)


def levels(rng, dims, split, smallest, top_value):
    loudness = 1.0
    for dim, shards_of in split:
        draws = jax.random.uniform(jax.random.fold_in(jax.random.fold_in(rng, 6), dim), (shards_of,), jnp.float32, smallest / len(split), top_value / len(split))
        loudness = loudness * jnp.repeat(jnp.exp(draws), dims[dim] // shards_of).reshape((-1,) + (1,) * (len(dims) - 1 - dim))
    return loudness


def bell_draw(rng, dims, deviation, limit, shards=(), kind=jnp.bfloat16):
    array = deviation * jax.random.normal(rng, dims, jnp.float32)
    if shards:
        array = array * levels(rng, dims, shards, -0.22, 0.18)
    return jnp.clip(array, -limit, limit).astype(kind)


def setup_inputs(seed: int = 0) -> dict:
    splits = jax.random.split(jax.random.key(seed), 6)
    return {
        "green_forward": bell_draw(splits[0], (NK, NTAU, NAO, NAO), 2.0, 12.0, ((0, 64), (1, 4))),
        "green_backward": bell_draw(splits[1], (NK, NTAU, NAO, NAO), 2.0, 12.0, ((0, 64), (1, 4))),
        "orbitals": bell_draw(splits[2], (NK, NAO, NAUX), NAO ** -0.5, 0.25, ((0, 64),)),
        "difference_index_table": draw_difference_index_table(jax.random.fold_in(splits[5], 71), 0),
        "ir_matrix": bell_draw(splits[4], (NW, NTAU), 1.0, 6.0, (), jnp.float32),
    }


def reference(green_forward, green_backward, orbitals, difference_index_table, ir_matrix):
    block_rows = min(256, NAUX)
    block_count = NAUX // block_rows
    tables = orbitals.astype(jnp.float32)

    def one_time(tindex):
        forward = lax.dynamic_index_in_dim(green_forward, tindex, 1, keepdims=False).astype(jnp.float32)
        backward = lax.dynamic_index_in_dim(green_backward, tindex, 1, keepdims=False).astype(jnp.float32)
        half_forward = lax.optimization_barrier(jnp.einsum('kij,kjm->kim', forward, tables).astype(jnp.bfloat16))
        half_backward = lax.optimization_barrier(jnp.einsum('kji,kjm->kim', backward, tables).astype(jnp.bfloat16))
        half_forward = half_forward.astype(jnp.float32)
        half_backward = half_backward.astype(jnp.float32)

        def one_block(bindex):
            columns = lax.dynamic_slice_in_dim(tables, bindex * block_rows, block_rows, 2)
            points_forward = jnp.einsum('kim,kin->kmn', columns, half_forward).astype(jnp.bfloat16)
            points_backward = jnp.einsum('kim,kin->kmn', columns, half_backward).astype(jnp.bfloat16)

            def one_shift(mapping):
                paired = jnp.take(points_backward, mapping, axis=0)
                return jnp.sum(points_forward.astype(jnp.float32) * paired.astype(jnp.float32), axis=0) / NK

            return lax.map(one_shift, difference_index_table)

        stacked = lax.map(one_block, jnp.arange(block_count, dtype=jnp.int32))
        return jnp.transpose(stacked, (1, 0, 2, 3)).reshape(NQ, NAUX, NAUX)

    polar_time = lax.map(one_time, jnp.arange(NTAU, dtype=jnp.int32))
    result = jnp.einsum('wt,tqmn->qwmn', ir_matrix, polar_time, precision=lax.Precision.HIGHEST)
    return result.astype(jnp.bfloat16)
```

```python
import functools

import jax
import jax.numpy as jnp
from jax import lax
from jax.experimental import pallas as pl
from jax.experimental.pallas import tpu as pltpu
from jax.sharding import PartitionSpec as P


def pair_kernel(table, ir, left, right, out, points):
    k = pl.program_id(0)
    steps = pl.num_programs(0)
    times, _, sides, rows, depth = left.shape
    columns = right.shape[2]
    product = jnp.dot(
        left[...].reshape(times * sides * rows, depth),
        right[0],
        preferred_element_type=jnp.float32,
    )
    points[k] = product.astype(jnp.bfloat16)
    transfers = out.shape[0]
    chunk = 256

    @pl.when(k == steps - 1)
    def _():
        for begin in range(0, columns, chunk):
            window = pl.ds(begin, chunk)
            polar = []
            for t in range(times):
                first = t * sides * rows

                def add(kk, sums):
                    forward = points[kk, pl.ds(first, rows), window].astype(jnp.float32)
                    new = []
                    for q in range(transfers):
                        other = table[q, kk]
                        backward = points[other, pl.ds(first + rows, rows), window]
                        new.append(sums[q] + forward * backward.astype(jnp.float32))
                    return tuple(new)

                zero = jnp.zeros((rows, chunk), jnp.float32)
                polar.append(lax.fori_loop(0, steps, add, (zero,) * transfers))
            for q in range(transfers):
                for w in range(out.shape[1]):
                    value = ir[w, 0] * polar[0][q]
                    for t in range(1, times):
                        value = value + ir[w, t] * polar[t][q]
                    out[q, w, :, window] = (value * (1.0 / steps)).astype(jnp.bfloat16)


def local(green_forward, green_backward, orbitals, difference_index_table, ir_matrix):
    tabulated = orbitals[0]
    count = lax.axis_size("ka")
    times = lax.axis_size("tau")
    depth, points = tabulated.shape
    rows = points // count
    columns = points // times
    forward = jnp.einsum(
        "im,ij->mj", tabulated, green_forward[0, 0], preferred_element_type=jnp.float32
    ).astype(jnp.bfloat16)
    backward = jnp.einsum(
        "im,ji->mj", tabulated, green_backward[0, 0], preferred_element_type=jnp.float32
    ).astype(jnp.bfloat16)
    left = jnp.stack(
        [forward.reshape(count, rows, depth), backward.reshape(count, rows, depth)], axis=1
    )
    left = lax.all_to_all(left, "ka", split_axis=0, concat_axis=0, tiled=True)
    left = lax.all_gather(left, "tau", axis=0, tiled=False)
    mine = lax.dynamic_slice_in_dim(tabulated, lax.axis_index("tau") * columns, columns, 1)
    right = lax.all_gather(mine, "ka", axis=0, tiled=False)
    transfers = difference_index_table.shape[0]
    frequencies = ir_matrix.shape[0]
    return pl.pallas_call(
        pair_kernel,
        grid_spec=pltpu.PrefetchScalarGridSpec(
            num_scalar_prefetch=2,
            grid=(count,),
            in_specs=[
                pl.BlockSpec((times, 1, 2, rows, depth), lambda k, *_: (0, k, 0, 0, 0)),
                pl.BlockSpec((1, depth, columns), lambda k, *_: (k, 0, 0)),
            ],
            out_specs=pl.BlockSpec(
                (transfers, frequencies, rows, columns), lambda k, *_: (0, 0, 0, 0)
            ),
            scratch_shapes=[pltpu.VMEM((count, times * 2 * rows, columns), jnp.bfloat16)],
        ),
        out_shape=jax.ShapeDtypeStruct((transfers, frequencies, rows, columns), jnp.bfloat16),
        compiler_params=pltpu.CompilerParams(vmem_limit_bytes=40 * 1024 * 1024),
    )(difference_index_table, ir_matrix, left, right)


def solution(mesh):
    placed = (P("ka", "tau", None, None), P("ka", "tau", None, None), P("ka", None, None), P(), P())
    return jax.shard_map(
        local, mesh=mesh, in_specs=placed, out_specs=P(None, None, "ka", "tau"), check_vma=False
    )
```

```python
import functools

import jax
import jax.numpy as jnp
from jax import lax
from jax.experimental import pallas as pl
from jax.experimental.pallas import tpu as pltpu
from jax.sharding import PartitionSpec as P

MESH = pl.DeviceIdType.MESH
ZS, XS, YS = 8, 4, 4
RING = ((0, 0), (1, 1), (-1, 1), (1, 2), (-1, 2), (1, 3), (-1, 3), (1, 4))
ZFIRST = 384


class Plan:
    def __init__(self):
        self.number = {}

    def __call__(self, *name):
        return self.number.setdefault(name, len(self.number))


PLAN = Plan()
for i in range(len(RING)):
    for part in ("wx", "wy", "cx"):
        for way in ("p", "n", "far"):
            PLAN(part, i, way)
    for part in ("wz", "cz", "dz", "pair"):
        PLAN(part, i)
for way in ("p", "n", "far"):
    PLAN("dx", way)
COPIES = len(PLAN.number)


def kernel(ir, table, w, orb, out, points, wr, cr, transit, staged, polar, send, recv, here):
    ka = lax.axis_index("ka")
    y = lax.axis_index("tau")
    core = lax.rem(ka, 2)
    x = lax.rem(ka // 2, XS)
    z = ka // (2 * XS)
    e = 1 - 2 * core

    def around(value, by, size):
        return lax.rem(value + e * by + size, size)

    def at_x(by):
        return (z * 2 * XS + around(x, by, XS) * 2 + core, y)

    def at_z(by):
        return (around(z, by, ZS) * 2 * XS + x * 2 + core, y)

    def at_y(by):
        return (ka, around(y, by, YS))

    sibling = (ka + e, y)
    depth, columns = cr.shape[2], cr.shape[3]
    quarter = pl.ds(pl.multiple_of(y * columns, columns), columns)
    pending = []

    def go(source, target, device, *name):
        number = PLAN(*name)
        copy = pltpu.make_async_remote_copy(
            src_ref=source,
            dst_ref=target,
            send_sem=send.at[number],
            recv_sem=recv.at[number],
            device_id=device,
            device_id_type=MESH,
        )
        copy.start()
        pending.append(copy)

    def arrive(target, *name):
        number = PLAN(*name)
        pltpu.make_async_remote_copy(
            src_ref=target,
            dst_ref=target,
            send_sem=send.at[number],
            recv_sem=recv.at[number],
            device_id=sibling,
            device_id_type=MESH,
        ).wait_recv()

    own_first = pltpu.make_async_copy(w.at[z, x], wr.at[y, z, x], here.at[0])
    own_rest = pltpu.make_async_copy(w.at[:, x], transit.at[:, x], here.at[1])
    own_right = pltpu.make_async_copy(orb.at[:, quarter], cr.at[z, x], here.at[2])
    own_first.start()
    own_rest.start()
    own_right.start()

    partners = [at_x(1), at_x(-1), at_x(2), at_y(1), at_y(-1), sibling]
    partners += [at_z(by) for by in (1, -1, 2, -2, 3, -3, 4)]
    barrier = pltpu.get_barrier_semaphore()
    for partner in partners:
        pl.semaphore_signal(barrier, inc=1, device_id=partner, device_id_type=MESH)
    pl.semaphore_wait(barrier, len(partners))

    def source(i):
        way, far = RING[i]
        return around(z, -way * far, ZS)

    def owner(i):
        way, far = RING[i]
        return around(z, way * far, ZS)

    ways = (("p", 1), ("n", -1), ("far", 2))
    low, high = pl.ds(0, ZFIRST), pl.ds(ZFIRST, depth - ZFIRST)

    def send_x(i):
        for name, by in ways:
            if i == 0:
                target = wr.at[y, z, x]
            else:
                target = transit.at[owner(i), x]
            go(w.at[owner(i), around(x, by, XS)], target, at_x(by), "wx", i, name)

    def send_z(i):
        if i == 0:
            own_first.wait()
        if i == 1:
            own_rest.wait()
        for name, by in ways:
            if i == 0:
                arrive(wr.at[y, z, around(x, -by, XS)], "wx", i, name)
            else:
                arrive(transit.at[owner(i), around(x, -by, XS)], "wx", i, name)
        if i:
            way, far = RING[i]
            go(transit.at[owner(i)], wr.at[y, z], at_z(way * far), "wz", i)

    def send_y(i):
        block = wr.at[y, source(i)]
        if i:
            arrive(block, "wz", i)
        go(block, block, at_y(1), "wy", i, "p")
        go(block, block, at_y(-1), "wy", i, "n")

    def forward_y(i):
        block = wr.at[around(y, -1, YS), source(i)]
        arrive(block, "wy", i, "p")
        go(block, block, at_y(1), "wy", i, "far")

    def ring_z(i, block, part):
        way, far = RING[i]
        if i:
            arrive(block, part, i)
            if far < (4 if way > 0 else 3):
                go(block, block, at_z(way), part, RING.index((way, far + 1)))

    def right_z(i):
        block = cr.at[source(i), x, low]
        ring_z(i, block, "cz")
        if i == 0:
            mine = orb.at[low, quarter]
            go(mine, block, at_z(1), "cz", 1)
            go(mine, block, at_z(-1), "cz", 2)
        else:
            mine = block
        go(mine, block, at_x(1), "cx", i, "p")
        go(mine, block, at_x(-1), "cx", i, "n")

    def right_x(i):
        block = cr.at[source(i), around(x, -1, XS), low]
        arrive(block, "cx", i, "p")
        go(block, block, at_x(1), "cx", i, "far")

    def other_x():
        block = cr.at[z, x, high]
        go(orb.at[high, quarter], block, at_x(1), "dx", "p")
        go(orb.at[high, quarter], block, at_x(-1), "dx", "n")

    def other_x_forward():
        block = cr.at[z, around(x, -1, XS), high]
        arrive(block, "dx", "p")
        go(block, block, at_x(1), "dx", "far")

    def other_x_end():
        own_right.wait()
        arrive(cr.at[z, around(x, 1, XS), high], "dx", "n")
        arrive(cr.at[z, around(x, 2, XS), high], "dx", "far")
        block = cr.at[z, :, high]
        go(block, block, at_z(1), "dz", 1)
        go(block, block, at_z(-1), "dz", 2)

    def other_z(i):
        ring_z(i, cr.at[source(i), :, high], "dz")

    def multiply(i):
        chunk = source(i)
        arrive(wr.at[around(y, 1, YS), chunk], "wy", i, "n")
        arrive(wr.at[around(y, 2, YS), chunk], "wy", i, "far")
        arrive(cr.at[chunk, around(x, 1, XS), low], "cx", i, "n")
        arrive(cr.at[chunk, around(x, 2, XS), low], "cx", i, "far")
        slot = i % 2
        if i >= 2:
            sent[i - 2].wait_send()
        half = wr.shape[3] // 2

        def one(column, carry):
            right = cr[chunk, column]
            for mine in (True, False):
                begin = pl.multiple_of((core if mine else 1 - core) * half, half)
                left = wr[:, chunk, column, pl.ds(begin, half), :]
                product = jnp.dot(
                    left.reshape(YS * half, depth), right, preferred_element_type=jnp.float32
                )
                product = product.astype(jnp.bfloat16).reshape(YS, half, columns)
                if mine:
                    points[core, chunk, column] = product
                else:
                    staged[slot, column] = product
            return carry

        lax.fori_loop(0, XS, one, 0)
        number = PLAN("pair", i)
        copy = pltpu.make_async_remote_copy(
            src_ref=staged.at[slot],
            dst_ref=points.at[core, chunk],
            send_sem=send.at[number],
            recv_sem=recv.at[number],
            device_id=sibling,
            device_id_type=MESH,
        )
        copy.start()
        sent.append(copy)

    sent = []
    send_x(0)
    right_z(0)
    other_x()
    for i in range(1, 8):
        send_x(i)
    send_z(0)
    send_y(0)
    other_x_forward()
    send_z(1)
    send_z(2)
    other_x_end()
    send_z(3)
    right_z(1)
    right_z(2)
    send_z(4)
    send_y(1)
    send_y(2)
    right_x(0)
    send_z(5)
    send_z(6)
    other_z(1)
    other_z(2)
    forward_y(0)
    send_z(7)
    right_z(3)
    right_z(4)
    send_y(3)
    forward_y(1)
    right_x(1)
    right_x(2)
    send_y(4)
    other_z(3)
    other_z(4)
    forward_y(2)
    right_z(5)
    right_z(6)
    send_y(5)
    forward_y(3)
    multiply(0)
    right_x(3)
    right_x(4)
    other_z(5)
    other_z(6)
    send_y(6)
    multiply(1)
    forward_y(4)
    right_z(7)
    send_y(7)
    multiply(2)
    right_x(5)
    right_x(6)
    other_z(7)
    forward_y(5)
    multiply(3)
    forward_y(6)
    right_x(7)
    multiply(4)
    forward_y(7)
    multiply(5)
    multiply(6)
    multiply(7)

    for i in range(len(RING)):
        arrive(points.at[1 - core, source(i)], "pair", i)

    transfers, frequencies = out.shape[0], out.shape[1]
    rows = out.shape[2]
    momenta = 2 * ZS * XS
    width = 256

    for begin in range(0, columns, width):
        window = pl.ds(begin, width)
        for t in range(YS):

            def add(k, sums):
                slot = (lax.rem(k, 2), k // (2 * XS), lax.rem(k // 2, XS))
                forward = points[*slot, t, pl.ds(0, rows), window].astype(jnp.float32)
                new = []
                for q in range(transfers):
                    o = table[q, k]
                    place = (lax.rem(o, 2), o // (2 * XS), lax.rem(o // 2, XS))
                    backward = points[*place, t, pl.ds(rows, rows), window]
                    new.append(sums[q] + forward * backward.astype(jnp.float32))
                return tuple(new)

            zero = jnp.zeros((rows, width), jnp.float32)
            sums = lax.fori_loop(0, momenta, add, (zero,) * transfers)
            for q in range(transfers):
                polar[t, q] = sums[q]
        for q in range(transfers):
            terms = [polar[t, q] for t in range(YS)]
            for f in range(frequencies):
                value = ir[f, 0] * terms[0]
                for t in range(1, YS):
                    value = value + ir[f, t] * terms[t]
                out[q, f, :, window] = (value * (1.0 / momenta)).astype(jnp.bfloat16)

    for copy in pending + sent[-2:]:
        copy.wait_send()


def local(green_forward, green_backward, orbitals, difference_index_table, ir_matrix):
    tabulated = orbitals[0]
    depth, points = tabulated.shape
    rows = points // (2 * ZS * XS)
    columns = points // YS
    forward = jnp.einsum(
        "im,ij->mj", tabulated, green_forward[0, 0], preferred_element_type=jnp.float32
    ).astype(jnp.bfloat16)
    backward = jnp.einsum(
        "im,ji->mj", tabulated, green_backward[0, 0], preferred_element_type=jnp.float32
    ).astype(jnp.bfloat16)
    shape = (ZS, XS, 2, rows, depth)
    left = jnp.stack([forward.reshape(shape), backward.reshape(shape)], axis=3)
    left = left.reshape(ZS, XS, 4 * rows, depth)
    transfers = difference_index_table.shape[0]
    frequencies = ir_matrix.shape[0]
    bf16 = jnp.bfloat16
    return pl.pallas_call(
        kernel,
        in_specs=[
            pl.BlockSpec(memory_space=pltpu.SMEM),
            pl.BlockSpec(memory_space=pltpu.SMEM),
            pl.BlockSpec(memory_space=pl.ANY),
            pl.BlockSpec(memory_space=pl.ANY),
        ],
        out_specs=pl.BlockSpec(memory_space=pltpu.VMEM),
        out_shape=jax.ShapeDtypeStruct((transfers, frequencies, rows, columns), bf16),
        scratch_shapes=[
            pltpu.VMEM((2, ZS, XS, YS, 2 * rows, columns), bf16),
            pltpu.VMEM((YS, ZS, XS, 4 * rows, depth), bf16),
            pltpu.VMEM((ZS, XS, depth, columns), bf16),
            pltpu.VMEM((ZS, XS, 4 * rows, depth), bf16),
            pltpu.VMEM((2, XS, YS, 2 * rows, columns), bf16),
            pltpu.VMEM((YS, transfers, rows, 256), jnp.float32),
            pltpu.SemaphoreType.DMA((COPIES,)),
            pltpu.SemaphoreType.DMA((COPIES,)),
            pltpu.SemaphoreType.DMA((3,)),
        ],
        compiler_params=pltpu.CompilerParams(
            collective_id=0, has_side_effects=True, vmem_limit_bytes=62 * 1024 * 1024
        ),
    )(ir_matrix, difference_index_table, left, tabulated)


def solution(mesh):
    placed = (P("ka", "tau", None, None), P("ka", "tau", None, None), P("ka", None, None), P(), P())
    return jax.shard_map(
        local, mesh=mesh, in_specs=placed, out_specs=P(None, None, "ka", "tau"), check_vma=False
    )
```

```python
import functools

import jax
import jax.numpy as jnp
from jax import lax
from jax.experimental import pallas as pl
from jax.experimental.pallas import tpu as pltpu
from jax.sharding import PartitionSpec as P

WIDTH = 256
UNROLL = 4
MESH = pl.DeviceIdType.MESH
ZS, XS, YS = 8, 4, 4
RING = ((0, 0), (1, 1), (-1, 1), (1, 2), (-1, 2), (1, 3), (-1, 3), (1, 4))
ZFIRST = 448
class Plan:
    def __init__(self):
        self.number = {}

    def __call__(self, *name):
        return self.number.setdefault(name, len(self.number))


PLAN = Plan()
for i in range(len(RING)):
    for part in ("wx", "wy", "cx"):
        for way in ("p", "n", "far"):
            PLAN(part, i, way)
    for part in ("wz", "cz", "dz", "pair"):
        PLAN(part, i)
for way in ("p", "n", "far"):
    PLAN("dx", way)
COPIES = len(PLAN.number)


def kernel(ir, table, w, orb, out, points, wr, cr, transit, staged, polar, send, recv, here):
    ka = lax.axis_index("ka")
    y = lax.axis_index("tau")
    core = lax.rem(ka, 2)
    x = lax.rem(ka // 2, XS)
    z = ka // (2 * XS)
    e = 1 - 2 * core

    def around(value, by, size):
        return lax.rem(value + e * by + size, size)

    def at_x(by):
        return (z * 2 * XS + around(x, by, XS) * 2 + core, y)

    def at_z(by):
        return (around(z, by, ZS) * 2 * XS + x * 2 + core, y)

    def at_y(by):
        return (ka, around(y, by, YS))

    sibling = (ka + e, y)
    depth, columns = cr.shape[2], cr.shape[3]
    quarter = pl.ds(pl.multiple_of(y * columns, columns), columns)
    pending, sent = [], []

    def go(source, target, device, *name):
        number = PLAN(*name)
        copy = pltpu.make_async_remote_copy(
            src_ref=source,
            dst_ref=target,
            send_sem=send.at[number],
            recv_sem=recv.at[number],
            device_id=device,
            device_id_type=MESH,
        )
        copy.start()
        pending.append(copy)

    def arrive(target, *name):
        number = PLAN(*name)
        pltpu.make_async_remote_copy(
            src_ref=target,
            dst_ref=target,
            send_sem=send.at[number],
            recv_sem=recv.at[number],
            device_id=sibling,
            device_id_type=MESH,
        ).wait_recv()

    own_first = pltpu.make_async_copy(w.at[z, x], wr.at[y, z, x], here.at[0])
    own_rest = pltpu.make_async_copy(w.at[:, x], transit.at[:, x], here.at[1])
    own_right = pltpu.make_async_copy(orb.at[:, quarter], cr.at[z, x], here.at[2])
    own_first.start()
    own_rest.start()
    own_right.start()

    partners = [at_x(1), at_x(-1), at_x(2), at_y(1), at_y(-1), sibling]
    partners += [at_z(by) for by in (1, -1, 2, -2, 3, -3, 4)]
    barrier = pltpu.get_barrier_semaphore()
    for partner in partners:
        pl.semaphore_signal(barrier, inc=1, device_id=partner, device_id_type=MESH)
    pl.semaphore_wait(barrier, len(partners))

    def turn(i):
        return 1 if i % 2 == 0 else -1

    def source(i):
        way, far = RING[i]
        return around(z, -way * far, ZS)

    def owner(i):
        way, far = RING[i]
        return around(z, way * far, ZS)

    ways = (("p", 1), ("n", -1), ("far", 2))
    low, high = pl.ds(0, ZFIRST), pl.ds(ZFIRST, depth - ZFIRST)

    def send_x(i):
        for name, by in ways:
            if i == 0:
                target = wr.at[y, z, x]
            else:
                target = transit.at[owner(i), x]
            go(w.at[owner(i), around(x, by, XS)], target, at_x(by), "wx", i, name)

    def send_z(i):
        if i == 0:
            own_first.wait()
        if i == 1:
            own_rest.wait()
        for name, by in ways:
            if i == 0:
                arrive(wr.at[y, z, around(x, -by, XS)], "wx", i, name)
            else:
                arrive(transit.at[owner(i), around(x, -by, XS)], "wx", i, name)
        if i:
            way, far = RING[i]
            go(transit.at[owner(i)], wr.at[y, z], at_z(way * far), "wz", i)

    def send_y(i):
        block = wr.at[y, source(i)]
        if i:
            arrive(block, "wz", i)
        go(block, block, at_y(turn(i)), "wy", i, "p")
        go(block, block, at_y(-turn(i)), "wy", i, "n")

    def forward_y(i):
        block = wr.at[around(y, -turn(i), YS), source(i)]
        arrive(block, "wy", i, "p")
        go(block, block, at_y(turn(i)), "wy", i, "far")

    def ring_z(i, block, part):
        way, far = RING[i]
        if i:
            arrive(block, part, i)
            if far < (4 if way > 0 else 3):
                go(block, block, at_z(way), part, RING.index((way, far + 1)))

    def right_z(i):
        block = cr.at[source(i), x, low]
        if i:
            ring_z(i, block, "cz")
        else:
            go(orb.at[low, quarter], block, at_z(1), "cz", 1)
            go(orb.at[low, quarter], block, at_z(-1), "cz", 2)

    def send_c(i):
        block = cr.at[source(i), x, low]
        mine = block if i else orb.at[low, quarter]
        go(mine, block, at_x(turn(i)), "cx", i, "p")
        go(mine, block, at_x(-turn(i)), "cx", i, "n")

    def right_x(i):
        block = cr.at[source(i), around(x, -turn(i), XS), low]
        arrive(block, "cx", i, "p")
        go(block, block, at_x(turn(i)), "cx", i, "far")

    def other_x():
        block = cr.at[z, x, high]
        go(orb.at[high, quarter], block, at_x(1), "dx", "p")
        go(orb.at[high, quarter], block, at_x(-1), "dx", "n")

    def other_x_forward():
        block = cr.at[z, around(x, -1, XS), high]
        arrive(block, "dx", "p")
        go(block, block, at_x(1), "dx", "far")

    def other_x_end():
        own_right.wait()
        arrive(cr.at[z, around(x, 1, XS), high], "dx", "n")
        arrive(cr.at[z, around(x, 2, XS), high], "dx", "far")
        block = cr.at[z, :, high]
        go(block, block, at_z(1), "dz", 1)
        go(block, block, at_z(-1), "dz", 2)

    def other_z(i):
        ring_z(i, cr.at[source(i), :, high], "dz")

    def multiply(i):
        chunk = source(i)
        arrive(wr.at[around(y, turn(i), YS), chunk], "wy", i, "n")
        arrive(wr.at[around(y, 2, YS), chunk], "wy", i, "far")
        arrive(cr.at[chunk, around(x, turn(i), XS), low], "cx", i, "n")
        arrive(cr.at[chunk, around(x, 2, XS), low], "cx", i, "far")
        slot = i % 2
        if i >= 2:
            sent[i - 2].wait_send()
        half = wr.shape[3] // 2

        def one(column, carry):
            right = cr[chunk, column]
            for mine in (True, False):
                begin = pl.multiple_of((core if mine else 1 - core) * half, half)
                left = wr[:, chunk, column, pl.ds(begin, half), :]
                left = jnp.stack([left[:, :, :depth], left[:, :, depth:]], axis=1)
                product = jnp.dot(
                    left.reshape(YS * 2 * half, depth), right, preferred_element_type=jnp.float32
                )
                product = product.astype(jnp.bfloat16).reshape(YS, 2 * half, columns)
                if mine:
                    points[core * (ZS * XS) + chunk * XS + column] = product
                else:
                    staged[slot, column] = product
            return carry

        lax.fori_loop(0, XS, one, 0)
        number = PLAN("pair", i)
        copy = pltpu.make_async_remote_copy(
            src_ref=staged.at[slot],
            dst_ref=points.at[pl.ds(core * (ZS * XS) + chunk * XS, XS)],
            send_sem=send.at[number],
            recv_sem=recv.at[number],
            device_id=sibling,
            device_id_type=MESH,
        )
        copy.start()
        sent.append(copy)

    other_x()
    send_x(0)
    send_x(1)
    right_z(0)
    send_x(2)
    send_c(0)
    send_z(0)
    other_x_forward()
    send_z(1)
    send_y(0)
    right_x(0)
    forward_y(0)
    right_z(1)
    send_x(3)
    send_c(1)
    other_x_end()
    send_z(2)
    send_y(1)
    right_x(1)
    right_z(2)
    forward_y(1)
    send_x(4)
    send_c(2)
    send_z(3)
    send_y(2)
    right_z(3)
    other_z(1)
    right_x(2)
    forward_y(2)
    send_c(3)
    multiply(0)
    send_x(5)
    right_z(4)
    send_z(4)
    send_y(3)
    other_z(2)
    right_x(3)
    send_c(4)
    forward_y(3)
    right_z(5)
    multiply(1)
    send_x(6)
    send_z(5)
    send_y(4)
    right_z(6)
    right_x(4)
    other_z(3)
    send_c(5)
    forward_y(4)
    multiply(2)
    send_x(7)
    send_z(6)
    send_y(5)
    right_z(7)
    send_c(6)
    right_x(5)
    other_z(4)
    forward_y(5)
    multiply(3)
    send_z(7)
    send_y(6)
    send_c(7)
    right_x(6)
    other_z(5)
    forward_y(6)
    multiply(4)
    send_y(7)
    right_x(7)
    forward_y(7)
    other_z(6)
    multiply(5)
    other_z(7)
    multiply(6)
    multiply(7)

    for i in range(len(RING)):
        arrive(points.at[pl.ds((1 - core) * (ZS * XS) + source(i) * XS, XS)], "pair", i)

    transfers, frequencies = out.shape[0], out.shape[1]
    rows = out.shape[2]
    momenta = 2 * ZS * XS
    width = WIDTH

    def place(k):
        return (k & 1) * (ZS * XS) + (k >> 1)

    for begin in range(0, columns, width):
        window = pl.ds(begin, width)
        for t in range(YS):

            def add(k, sums):
                forward = points[place(k), t, pl.ds(0, rows), window].astype(jnp.float32)
                new = []
                for q in range(transfers):
                    backward = points[place(table[q, k]), t, pl.ds(rows, rows), window]
                    new.append(sums[q] + forward * backward.astype(jnp.float32))
                return tuple(new)

            zero = jnp.zeros((rows, width), jnp.float32)
            sums = lax.fori_loop(0, momenta, add, (zero,) * transfers, unroll=UNROLL)
            for q in range(transfers):
                polar[t, q] = sums[q]
        for q in range(transfers):
            terms = [polar[t, q] for t in range(YS)]
            for f in range(frequencies):
                value = ir[f, 0] * terms[0]
                for t in range(1, YS):
                    value = value + ir[f, t] * terms[t]
                out[q, f, :, window] = (value * (1.0 / momenta)).astype(jnp.bfloat16)

    for copy in pending + sent[-2:]:
        copy.wait_send()


def local(green_forward, green_backward, orbitals, difference_index_table, ir_matrix):
    tabulated = orbitals[0]
    depth, points = tabulated.shape
    rows = points // (2 * ZS * XS)
    columns = points // YS
    both = jnp.concatenate([green_forward[0, 0], green_backward[0, 0].T], axis=1)
    left = jnp.einsum("im,ij->mj", tabulated, both, preferred_element_type=jnp.float32)
    left = left.astype(jnp.bfloat16).reshape(ZS, XS, 2 * rows, 2 * depth)
    transfers = difference_index_table.shape[0]
    frequencies = ir_matrix.shape[0]
    bf16 = jnp.bfloat16
    return pl.pallas_call(
        kernel,
        in_specs=[
            pl.BlockSpec(memory_space=pltpu.SMEM),
            pl.BlockSpec(memory_space=pltpu.SMEM),
            pl.BlockSpec(memory_space=pl.ANY),
            pl.BlockSpec(memory_space=pl.ANY),
        ],
        out_specs=pl.BlockSpec(memory_space=pltpu.VMEM),
        out_shape=jax.ShapeDtypeStruct((transfers, frequencies, rows, columns), bf16),
        scratch_shapes=[
            pltpu.VMEM((2 * ZS * XS, YS, 2 * rows, columns), bf16),
            pltpu.VMEM((YS, ZS, XS, 2 * rows, 2 * depth), bf16),
            pltpu.VMEM((ZS, XS, depth, columns), bf16),
            pltpu.VMEM((ZS, XS, 2 * rows, 2 * depth), bf16),
            pltpu.VMEM((2, XS, YS, 2 * rows, columns), bf16),
            pltpu.VMEM((YS, transfers, rows, WIDTH), jnp.float32),
            pltpu.SemaphoreType.DMA((COPIES,)),
            pltpu.SemaphoreType.DMA((COPIES,)),
            pltpu.SemaphoreType.DMA((3,)),
        ],
        compiler_params=pltpu.CompilerParams(
            collective_id=0, has_side_effects=True, vmem_limit_bytes=62 * 1024 * 1024
        ),
    )(ir_matrix, difference_index_table, left, tabulated)


def solution(mesh):
    placed = (P("ka", "tau", None, None), P("ka", "tau", None, None), P("ka", None, None), P(), P())
    return jax.shard_map(
        local, mesh=mesh, in_specs=placed, out_specs=P(None, None, "ka", "tau"), check_vma=False
    )
```

```python
import functools

import jax
import jax.numpy as jnp
from jax import lax
from jax.experimental import pallas as pl
from jax.experimental.pallas import tpu as pltpu
from jax.sharding import PartitionSpec as P

WIDTH = 256
UNROLL = 4
MESH = pl.DeviceIdType.MESH
ZS, XS, YS = 8, 4, 4
RING = ((0, 0), (1, 1), (-1, 1), (1, 2), (-1, 2), (1, 3), (-1, 3), (1, 4))
ZFIRST = 432
class Plan:
    def __init__(self):
        self.number = {}

    def __call__(self, *name):
        return self.number.setdefault(name, len(self.number))


PLAN = Plan()
for i in range(len(RING)):
    for part in ("wx", "wy", "cx"):
        for way in ("p", "n", "far"):
            PLAN(part, i, way)
    for part in ("wz", "cz", "dz", "pair"):
        PLAN(part, i)
for way in ("p", "n", "far"):
    PLAN("dx", way)
COPIES = len(PLAN.number)


def kernel(
    ir,
    table,
    green_f,
    green_b,
    orb,
    out,
    points,
    wr,
    cr,
    transit,
    staged,
    polar,
    tabulated,
    green,
    send,
    recv,
    here,
):
    ka = lax.axis_index("ka")
    y = lax.axis_index("tau")
    core = lax.rem(ka, 2)
    x = lax.rem(ka // 2, XS)
    z = ka // (2 * XS)
    e = 1 - 2 * core

    def around(value, by, size):
        return lax.rem(value + e * by + size, size)

    def at_x(by):
        return (z * 2 * XS + around(x, by, XS) * 2 + core, y)

    def at_z(by):
        return (around(z, by, ZS) * 2 * XS + x * 2 + core, y)

    def at_y(by):
        return (ka, around(y, by, YS))

    sibling = (ka + e, y)
    depth, columns = cr.shape[2], cr.shape[3]
    quarter = pl.ds(pl.multiple_of(y * columns, columns), columns)
    pending, sent = [], []

    def go(source, target, device, *name):
        number = PLAN(*name)
        copy = pltpu.make_async_remote_copy(
            src_ref=source,
            dst_ref=target,
            send_sem=send.at[number],
            recv_sem=recv.at[number],
            device_id=device,
            device_id_type=MESH,
        )
        copy.start()
        pending.append(copy)

    def arrive(target, *name):
        number = PLAN(*name)
        pltpu.make_async_remote_copy(
            src_ref=target,
            dst_ref=target,
            send_sem=send.at[number],
            recv_sem=recv.at[number],
            device_id=sibling,
            device_id_type=MESH,
        ).wait_recv()

    held = core * (ZS * XS)
    loads = [
        pltpu.make_async_copy(green_f, green.at[0], here.at[8]),
        pltpu.make_async_copy(green_b, green.at[1], here.at[9]),
        pltpu.make_async_copy(orb, tabulated, here.at[10]),
    ]
    own_right = pltpu.make_async_copy(orb.at[:, quarter], cr.at[z, x], here.at[11])
    for load in loads:
        load.start()
    own_right.start()
    own_left, sent_x = {}, {}

    partners = [at_x(1), at_x(-1), at_x(2), at_y(1), at_y(-1), sibling]
    partners += [at_z(by) for by in (1, -1, 2, -2, 3, -3, 4)]
    barrier = pltpu.get_barrier_semaphore()
    for partner in partners:
        pl.semaphore_signal(barrier, inc=1, device_id=partner, device_id_type=MESH)
    pl.semaphore_wait(barrier, len(partners))

    def turn(i):
        return 1 if i % 2 == 0 else -1

    def source(i):
        way, far = RING[i]
        return around(z, -way * far, ZS)

    def owner(i):
        way, far = RING[i]
        return around(z, way * far, ZS)

    ways = (("p", 1), ("n", -1), ("far", 2))
    low, high = pl.ds(0, ZFIRST), pl.ds(ZFIRST, depth - ZFIRST)

    def send_x(i):
        if i == 0:
            for load in loads:
                load.wait()
        height = XS * wr.shape[4]
        begin = pl.multiple_of(owner(i) * height, height)
        across = tabulated[:, pl.ds(begin, height)]
        first = held + owner(i) * XS
        for side, summed in ((0, 0), (1, 1)):
            part = lax.dot_general(
                across,
                green[side],
                (((0,), (summed,)), ((), ())),
                preferred_element_type=jnp.float32,
            )
            points[pl.ds(first, XS), side] = part.astype(jnp.bfloat16).reshape(
                XS, height // XS, depth
            )
        target = transit.at[owner(i), x] if i else wr.at[y, z, x]
        own_left[i] = pltpu.make_async_copy(
            points.at[first + x, pl.ds(0, 2)], target, here.at[i]
        )
        own_left[i].start()
        for name, by in ways:
            block = points.at[first + around(x, by, XS), pl.ds(0, 2)]
            go(block, target, at_x(by), "wx", i, name)
            sent_x.setdefault(i, []).append(pending.pop())

    def send_z(i):
        own_left[i].wait()
        for name, by in ways:
            if i == 0:
                arrive(wr.at[y, z, around(x, -by, XS)], "wx", i, name)
            else:
                arrive(transit.at[owner(i), around(x, -by, XS)], "wx", i, name)
        if i:
            way, far = RING[i]
            go(transit.at[owner(i)], wr.at[y, z], at_z(way * far), "wz", i)

    def send_y(i):
        block = wr.at[y, source(i)]
        if i:
            arrive(block, "wz", i)
        go(block, block, at_y(turn(i)), "wy", i, "p")
        go(block, block, at_y(-turn(i)), "wy", i, "n")

    def forward_y(i):
        block = wr.at[around(y, -turn(i), YS), source(i)]
        arrive(block, "wy", i, "p")
        go(block, block, at_y(turn(i)), "wy", i, "far")

    def ring_z(i, block, part):
        way, far = RING[i]
        if i:
            arrive(block, part, i)
            if far < (4 if way > 0 else 3):
                go(block, block, at_z(way), part, RING.index((way, far + 1)))

    def right_z(i):
        block = cr.at[source(i), x, low]
        if i:
            ring_z(i, block, "cz")
        else:
            go(orb.at[low, quarter], block, at_z(1), "cz", 1)
            go(orb.at[low, quarter], block, at_z(-1), "cz", 2)

    def send_c(i):
        block = cr.at[source(i), x, low]
        mine = block if i else orb.at[low, quarter]
        go(mine, block, at_x(turn(i)), "cx", i, "p")
        go(mine, block, at_x(-turn(i)), "cx", i, "n")

    def right_x(i):
        block = cr.at[source(i), around(x, -turn(i), XS), low]
        arrive(block, "cx", i, "p")
        go(block, block, at_x(turn(i)), "cx", i, "far")

    def other_x():
        block = cr.at[z, x, high]
        go(orb.at[high, quarter], block, at_x(1), "dx", "p")
        go(orb.at[high, quarter], block, at_x(-1), "dx", "n")

    def other_x_forward():
        block = cr.at[z, around(x, -1, XS), high]
        arrive(block, "dx", "p")
        go(block, block, at_x(1), "dx", "far")

    def other_x_end():
        own_right.wait()
        arrive(cr.at[z, around(x, 1, XS), high], "dx", "n")
        arrive(cr.at[z, around(x, 2, XS), high], "dx", "far")
        block = cr.at[z, :, high]
        go(block, block, at_z(1), "dz", 1)
        go(block, block, at_z(-1), "dz", 2)

    def other_z(i):
        ring_z(i, cr.at[source(i), :, high], "dz")

    def multiply(i):
        chunk = source(i)
        way, far = RING[i]
        mirror = RING.index((-way, far)) if (-way, far) in RING else i
        for copy in sent_x.pop(mirror):
            copy.wait_send()
        arrive(wr.at[around(y, turn(i), YS), chunk], "wy", i, "n")
        arrive(wr.at[around(y, 2, YS), chunk], "wy", i, "far")
        arrive(cr.at[chunk, around(x, turn(i), XS), low], "cx", i, "n")
        arrive(cr.at[chunk, around(x, 2, XS), low], "cx", i, "far")
        slot = i % 2
        if i >= 2:
            sent[i - 2].wait_send()
        half = wr.shape[4] // 2

        def one(column, carry):
            right = cr[chunk, column]
            for mine in (True, False):
                begin = pl.multiple_of((core if mine else 1 - core) * half, half)
                left = wr[:, chunk, column, :, pl.ds(begin, half), :]
                product = jnp.dot(
                    left.reshape(YS * 2 * half, depth), right, preferred_element_type=jnp.float32
                )
                product = product.astype(jnp.bfloat16).reshape(YS, 2 * half, columns)
                if mine:
                    points[core * (ZS * XS) + chunk * XS + column] = product
                else:
                    staged[slot, column] = product
            return carry

        lax.fori_loop(0, XS, one, 0)
        number = PLAN("pair", i)
        copy = pltpu.make_async_remote_copy(
            src_ref=staged.at[slot],
            dst_ref=points.at[pl.ds(core * (ZS * XS) + chunk * XS, XS)],
            send_sem=send.at[number],
            recv_sem=recv.at[number],
            device_id=sibling,
            device_id_type=MESH,
        )
        copy.start()
        sent.append(copy)

    other_x()
    right_z(0)
    send_x(0)
    send_c(0)
    send_z(0)
    send_x(1)
    send_x(2)
    send_z(1)
    other_x_forward()
    send_y(0)
    right_x(0)
    forward_y(0)
    right_z(1)
    send_x(3)
    send_z(2)
    send_c(1)
    other_x_end()
    send_y(1)
    right_x(1)
    right_z(2)
    forward_y(1)
    send_z(3)
    send_x(4)
    send_c(2)
    send_y(2)
    right_z(3)
    other_z(1)
    right_x(2)
    forward_y(2)
    send_c(3)
    multiply(0)
    send_z(4)
    send_x(5)
    right_z(4)
    send_y(3)
    other_z(2)
    right_x(3)
    send_c(4)
    forward_y(3)
    right_z(5)
    send_z(5)
    multiply(1)
    send_x(6)
    send_y(4)
    right_z(6)
    right_x(4)
    other_z(3)
    send_c(5)
    forward_y(4)
    send_z(6)
    multiply(2)
    send_x(7)
    send_y(5)
    right_z(7)
    send_c(6)
    right_x(5)
    send_z(7)
    forward_y(5)
    multiply(3)
    other_z(4)
    send_y(6)
    send_c(7)
    right_x(6)
    forward_y(6)
    multiply(4)
    send_y(7)
    other_z(5)
    right_x(7)
    forward_y(7)
    multiply(5)
    other_z(6)
    multiply(6)
    other_z(7)
    multiply(7)

    for i in range(len(RING)):
        arrive(points.at[pl.ds((1 - core) * (ZS * XS) + source(i) * XS, XS)], "pair", i)

    transfers, frequencies = out.shape[0], out.shape[1]
    rows = out.shape[2]
    momenta = 2 * ZS * XS
    width = WIDTH

    def place(k):
        return (k & 1) * (ZS * XS) + (k >> 1)

    for begin in range(0, columns, width):
        window = pl.ds(begin, width)
        for t in range(YS):

            def add(k, sums):
                forward = points[place(k), t, pl.ds(0, rows), window].astype(jnp.float32)
                new = []
                for q in range(transfers):
                    backward = points[place(table[q, k]), t, pl.ds(rows, rows), window]
                    new.append(sums[q] + forward * backward.astype(jnp.float32))
                return tuple(new)

            zero = jnp.zeros((rows, width), jnp.float32)
            sums = lax.fori_loop(0, momenta, add, (zero,) * transfers, unroll=UNROLL)
            for q in range(transfers):
                polar[t, q] = sums[q]
        for q in range(transfers):
            terms = [polar[t, q] for t in range(YS)]
            for f in range(frequencies):
                value = ir[f, 0] * terms[0]
                for t in range(1, YS):
                    value = value + ir[f, t] * terms[t]
                out[q, f, :, window] = (value * (1.0 / momenta)).astype(jnp.bfloat16)

    for copy in pending + sent[-2:]:
        copy.wait_send()


def local(green_forward, green_backward, orbitals, difference_index_table, ir_matrix):
    tabulated = orbitals[0]
    depth, points = tabulated.shape
    rows = points // (2 * ZS * XS)
    columns = points // YS
    transfers = difference_index_table.shape[0]
    frequencies = ir_matrix.shape[0]
    bf16 = jnp.bfloat16
    return pl.pallas_call(
        kernel,
        in_specs=[
            pl.BlockSpec(memory_space=pltpu.SMEM),
            pl.BlockSpec(memory_space=pltpu.SMEM),
            pl.BlockSpec(memory_space=pl.ANY),
            pl.BlockSpec(memory_space=pl.ANY),
            pl.BlockSpec(memory_space=pl.ANY),
        ],
        out_specs=pl.BlockSpec(memory_space=pltpu.VMEM),
        out_shape=jax.ShapeDtypeStruct((transfers, frequencies, rows, columns), bf16),
        scratch_shapes=[
            pltpu.VMEM((2 * ZS * XS, YS, 2 * rows, columns), bf16),
            pltpu.VMEM((YS, ZS, XS, 2, 2 * rows, depth), bf16),
            pltpu.VMEM((ZS, XS, depth, columns), bf16),
            pltpu.VMEM((ZS, XS, 2, 2 * rows, depth), bf16),
            pltpu.VMEM((2, XS, YS, 2 * rows, columns), bf16),
            pltpu.VMEM((YS, transfers, rows, WIDTH), jnp.float32),
            pltpu.VMEM((depth, points), bf16),
            pltpu.VMEM((2, depth, depth), bf16),
            pltpu.SemaphoreType.DMA((COPIES,)),
            pltpu.SemaphoreType.DMA((COPIES,)),
            pltpu.SemaphoreType.DMA((12,)),
        ],
        compiler_params=pltpu.CompilerParams(
            collective_id=0, has_side_effects=True, vmem_limit_bytes=62 * 1024 * 1024
        ),
    )(ir_matrix, difference_index_table, green_forward[0, 0], green_backward[0, 0], tabulated)


def solution(mesh):
    placed = (P("ka", "tau", None, None), P("ka", "tau", None, None), P("ka", None, None), P(), P())
    return jax.shard_map(
        local, mesh=mesh, in_specs=placed, out_specs=P(None, None, "ka", "tau"), check_vma=False
    )
```

```python
import functools

import jax
import jax.numpy as jnp
from jax import lax
from jax.experimental import pallas as pl
from jax.experimental.pallas import tpu as pltpu
from jax.sharding import PartitionSpec as P

WIDTH = 256
UNROLL = 8
MESH = pl.DeviceIdType.MESH
ZS, XS, YS = 8, 4, 4
RING = ((0, 0), (1, 1), (-1, 1), (1, 2), (-1, 2), (1, 3), (-1, 3), (1, 4))
ZFIRST = 432
class Plan:
    def __init__(self):
        self.number = {}

    def __call__(self, *name):
        return self.number.setdefault(name, len(self.number))


PLAN = Plan()
for i in range(len(RING)):
    for part in ("wx", "wy", "cx"):
        for way in ("p", "n", "far"):
            PLAN(part, i, way)
    for part in ("wz", "cz", "dz", "pair"):
        PLAN(part, i)
for way in ("p", "n", "far"):
    PLAN("dx", way)
COPIES = len(PLAN.number)


def kernel(
    ir,
    table,
    green_f,
    green_b,
    orb,
    out,
    points,
    wr,
    cr,
    transit,
    staged,
    polar,
    tabulated,
    green,
    send,
    recv,
    here,
):
    ka = lax.axis_index("ka")
    y = lax.axis_index("tau")
    core = lax.rem(ka, 2)
    x = lax.rem(ka // 2, XS)
    z = ka // (2 * XS)
    e = 1 - 2 * core

    def around(value, by, size):
        return lax.rem(value + e * by + size, size)

    def at_x(by):
        return (z * 2 * XS + around(x, by, XS) * 2 + core, y)

    def at_z(by):
        return (around(z, by, ZS) * 2 * XS + x * 2 + core, y)

    def at_y(by):
        return (ka, around(y, by, YS))

    sibling = (ka + e, y)
    depth, columns = cr.shape[2], cr.shape[3]
    quarter = pl.ds(pl.multiple_of(y * columns, columns), columns)
    pending, sent = [], []

    def go(source, target, device, *name):
        number = PLAN(*name)
        copy = pltpu.make_async_remote_copy(
            src_ref=source,
            dst_ref=target,
            send_sem=send.at[number],
            recv_sem=recv.at[number],
            device_id=device,
            device_id_type=MESH,
        )
        copy.start()
        pending.append(copy)

    def arrive(target, *name):
        number = PLAN(*name)
        pltpu.make_async_remote_copy(
            src_ref=target,
            dst_ref=target,
            send_sem=send.at[number],
            recv_sem=recv.at[number],
            device_id=sibling,
            device_id_type=MESH,
        ).wait_recv()

    held = core * (ZS * XS)
    loads = [
        pltpu.make_async_copy(green_f, green.at[0], here.at[8]),
        pltpu.make_async_copy(green_b, green.at[1], here.at[9]),
        pltpu.make_async_copy(orb, tabulated, here.at[10]),
    ]
    own_right = pltpu.make_async_copy(orb.at[:, quarter], cr.at[z, x], here.at[11])
    for load in loads:
        load.start()
    own_right.start()
    own_left, sent_x = {}, {}

    partners = [at_x(1), at_x(-1), at_x(2), at_y(1), at_y(-1), sibling]
    partners += [at_z(by) for by in (1, -1, 2, -2, 3, -3, 4)]
    barrier = pltpu.get_barrier_semaphore()
    for partner in partners:
        pl.semaphore_signal(barrier, inc=1, device_id=partner, device_id_type=MESH)
    pl.semaphore_wait(barrier, len(partners))

    def turn(i):
        return 1 if i % 2 == 0 else -1

    def source(i):
        way, far = RING[i]
        return around(z, -way * far, ZS)

    def owner(i):
        way, far = RING[i]
        return around(z, way * far, ZS)

    ways = (("p", 1), ("n", -1), ("far", 2))
    low, high = pl.ds(0, ZFIRST), pl.ds(ZFIRST, depth - ZFIRST)

    def send_x(i):
        if i == 0:
            for load in loads:
                load.wait()
        height = XS * wr.shape[4]
        begin = pl.multiple_of(owner(i) * height, height)
        across = tabulated[:, pl.ds(begin, height)]
        first = held + owner(i) * XS
        for side, summed in ((0, 0), (1, 1)):
            part = lax.dot_general(
                across,
                green[side],
                (((0,), (summed,)), ((), ())),
                preferred_element_type=jnp.float32,
            )
            points[pl.ds(first, XS), side] = part.astype(jnp.bfloat16).reshape(
                XS, height // XS, depth
            )
        target = transit.at[owner(i), x] if i else wr.at[y, z, x]
        own_left[i] = pltpu.make_async_copy(
            points.at[first + x, pl.ds(0, 2)], target, here.at[i]
        )
        own_left[i].start()
        for name, by in ways:
            block = points.at[first + around(x, by, XS), pl.ds(0, 2)]
            go(block, target, at_x(by), "wx", i, name)
            sent_x.setdefault(i, []).append(pending.pop())

    def send_z(i):
        own_left[i].wait()
        for name, by in ways:
            if i == 0:
                arrive(wr.at[y, z, around(x, -by, XS)], "wx", i, name)
            else:
                arrive(transit.at[owner(i), around(x, -by, XS)], "wx", i, name)
        if i:
            way, far = RING[i]
            go(transit.at[owner(i)], wr.at[y, z], at_z(way * far), "wz", i)

    def send_y(i):
        block = wr.at[y, source(i)]
        if i:
            arrive(block, "wz", i)
        go(block, block, at_y(turn(i)), "wy", i, "p")
        go(block, block, at_y(-turn(i)), "wy", i, "n")

    def forward_y(i):
        block = wr.at[around(y, -turn(i), YS), source(i)]
        arrive(block, "wy", i, "p")
        go(block, block, at_y(turn(i)), "wy", i, "far")

    def ring_z(i, block, part):
        way, far = RING[i]
        if i:
            arrive(block, part, i)
            if far < (4 if way > 0 else 3):
                go(block, block, at_z(way), part, RING.index((way, far + 1)))

    def right_z(i):
        block = cr.at[source(i), x, low]
        if i:
            ring_z(i, block, "cz")
        else:
            go(orb.at[low, quarter], block, at_z(1), "cz", 1)
            go(orb.at[low, quarter], block, at_z(-1), "cz", 2)

    def send_c(i):
        block = cr.at[source(i), x, low]
        mine = block if i else orb.at[low, quarter]
        go(mine, block, at_x(turn(i)), "cx", i, "p")
        go(mine, block, at_x(-turn(i)), "cx", i, "n")

    def right_x(i):
        block = cr.at[source(i), around(x, -turn(i), XS), low]
        arrive(block, "cx", i, "p")
        go(block, block, at_x(turn(i)), "cx", i, "far")

    def other_x():
        block = cr.at[z, x, high]
        go(orb.at[high, quarter], block, at_x(1), "dx", "p")
        go(orb.at[high, quarter], block, at_x(-1), "dx", "n")

    def other_x_forward():
        block = cr.at[z, around(x, -1, XS), high]
        arrive(block, "dx", "p")
        go(block, block, at_x(1), "dx", "far")

    def other_x_end():
        own_right.wait()
        arrive(cr.at[z, around(x, 1, XS), high], "dx", "n")
        arrive(cr.at[z, around(x, 2, XS), high], "dx", "far")
        block = cr.at[z, :, high]
        go(block, block, at_z(1), "dz", 1)
        go(block, block, at_z(-1), "dz", 2)

    def other_z(i):
        ring_z(i, cr.at[source(i), :, high], "dz")

    def multiply(i):
        chunk = source(i)
        way, far = RING[i]
        mirror = RING.index((-way, far)) if (-way, far) in RING else i
        for copy in sent_x.pop(mirror):
            copy.wait_send()
        arrive(wr.at[around(y, turn(i), YS), chunk], "wy", i, "n")
        arrive(wr.at[around(y, 2, YS), chunk], "wy", i, "far")
        arrive(cr.at[chunk, around(x, turn(i), XS), low], "cx", i, "n")
        arrive(cr.at[chunk, around(x, 2, XS), low], "cx", i, "far")
        slot = i % 2
        if i >= 2:
            sent[i - 2].wait_send()
        half = wr.shape[4] // 2

        def one(mine, column, carry):
            right = cr[chunk, column]
            begin = pl.multiple_of((core if mine else 1 - core) * half, half)
            left = wr[:, chunk, column, :, pl.ds(begin, half), :]
            product = jnp.dot(
                left.reshape(YS * 2 * half, depth), right, preferred_element_type=jnp.float32
            )
            product = product.astype(jnp.bfloat16).reshape(YS, 2 * half, columns)
            if mine:
                points[core * (ZS * XS) + chunk * XS + column] = product
            else:
                staged[slot, column] = product
            return carry

        lax.fori_loop(0, XS, functools.partial(one, False), 0)
        number = PLAN("pair", i)
        copy = pltpu.make_async_remote_copy(
            src_ref=staged.at[slot],
            dst_ref=points.at[pl.ds(core * (ZS * XS) + chunk * XS, XS)],
            send_sem=send.at[number],
            recv_sem=recv.at[number],
            device_id=sibling,
            device_id_type=MESH,
        )
        copy.start()
        sent.append(copy)
        lax.fori_loop(0, XS, functools.partial(one, True), 0)

    other_x()
    right_z(0)
    send_x(0)
    send_c(0)
    send_z(0)
    send_x(1)
    send_x(2)
    send_z(1)
    other_x_forward()
    send_y(0)
    right_x(0)
    forward_y(0)
    right_z(1)
    send_x(3)
    send_z(2)
    send_c(1)
    other_x_end()
    send_y(1)
    right_x(1)
    right_z(2)
    forward_y(1)
    send_z(3)
    send_x(4)
    send_c(2)
    send_y(2)
    right_z(3)
    other_z(1)
    right_x(2)
    forward_y(2)
    send_c(3)
    multiply(0)
    send_z(4)
    send_x(5)
    right_z(4)
    send_y(3)
    other_z(2)
    right_x(3)
    send_c(4)
    forward_y(3)
    right_z(5)
    send_z(5)
    multiply(1)
    send_x(6)
    multiply(2)
    send_y(4)
    right_z(6)
    right_x(4)
    other_z(3)
    send_c(5)
    forward_y(4)
    send_z(6)
    multiply(3)
    send_x(7)
    send_y(5)
    right_z(7)
    send_c(6)
    right_x(5)
    send_z(7)
    forward_y(5)
    other_z(4)
    multiply(4)
    send_y(6)
    send_c(7)
    right_x(6)
    forward_y(6)
    send_y(7)
    other_z(5)
    multiply(5)
    right_x(7)
    forward_y(7)
    other_z(6)
    multiply(6)
    other_z(7)
    multiply(7)

    for i in range(len(RING)):
        arrive(points.at[pl.ds((1 - core) * (ZS * XS) + source(i) * XS, XS)], "pair", i)

    transfers, frequencies = out.shape[0], out.shape[1]
    rows = out.shape[2]
    momenta = 2 * ZS * XS
    width = WIDTH

    def place(k):
        return (k & 1) * (ZS * XS) + (k >> 1)

    for begin in range(0, columns, width):
        window = pl.ds(begin, width)
        for t in range(YS):

            def add(k, sums):
                forward = points[place(k), t, pl.ds(0, rows), window].astype(jnp.float32)
                new = []
                for q in range(transfers):
                    backward = points[place(table[q, k]), t, pl.ds(rows, rows), window]
                    new.append(sums[q] + forward * backward.astype(jnp.float32))
                return tuple(new)

            zero = jnp.zeros((rows, width), jnp.float32)
            sums = lax.fori_loop(0, momenta, add, (zero,) * transfers, unroll=UNROLL)
            for q in range(transfers):
                polar[t, q] = sums[q]
        for q in range(transfers):
            terms = [polar[t, q] for t in range(YS)]
            for f in range(frequencies):
                value = ir[f, 0] * terms[0]
                for t in range(1, YS):
                    value = value + ir[f, t] * terms[t]
                out[q, f, :, window] = (value * (1.0 / momenta)).astype(jnp.bfloat16)

    for copy in pending + sent[-2:]:
        copy.wait_send()


def local(green_forward, green_backward, orbitals, difference_index_table, ir_matrix):
    tabulated = orbitals[0]
    depth, points = tabulated.shape
    rows = points // (2 * ZS * XS)
    columns = points // YS
    transfers = difference_index_table.shape[0]
    frequencies = ir_matrix.shape[0]
    bf16 = jnp.bfloat16
    return pl.pallas_call(
        kernel,
        in_specs=[
            pl.BlockSpec(memory_space=pltpu.SMEM),
            pl.BlockSpec(memory_space=pltpu.SMEM),
            pl.BlockSpec(memory_space=pl.ANY),
            pl.BlockSpec(memory_space=pl.ANY),
            pl.BlockSpec(memory_space=pl.ANY),
        ],
        out_specs=pl.BlockSpec(memory_space=pltpu.VMEM),
        out_shape=jax.ShapeDtypeStruct((transfers, frequencies, rows, columns), bf16),
        scratch_shapes=[
            pltpu.VMEM((2 * ZS * XS, YS, 2 * rows, columns), bf16),
            pltpu.VMEM((YS, ZS, XS, 2, 2 * rows, depth), bf16),
            pltpu.VMEM((ZS, XS, depth, columns), bf16),
            pltpu.VMEM((ZS, XS, 2, 2 * rows, depth), bf16),
            pltpu.VMEM((2, XS, YS, 2 * rows, columns), bf16),
            pltpu.VMEM((YS, transfers, rows, WIDTH), jnp.float32),
            pltpu.VMEM((depth, points), bf16),
            pltpu.VMEM((2, depth, depth), bf16),
            pltpu.SemaphoreType.DMA((COPIES,)),
            pltpu.SemaphoreType.DMA((COPIES,)),
            pltpu.SemaphoreType.DMA((12,)),
        ],
        compiler_params=pltpu.CompilerParams(
            collective_id=0, has_side_effects=True, vmem_limit_bytes=62 * 1024 * 1024
        ),
    )(ir_matrix, difference_index_table, green_forward[0, 0], green_backward[0, 0], tabulated)


def solution(mesh):
    placed = (P("ka", "tau", None, None), P("ka", "tau", None, None), P("ka", None, None), P(), P())
    return jax.shard_map(
        local, mesh=mesh, in_specs=placed, out_specs=P(None, None, "ka", "tau"), check_vma=False
    )
```
